128 devices in a mesh: blk: 16 (over x_hi, z, core), dom: 8 (over x_lo, y).
Axes of the slice: x: 4 (x_hi: 2, x_lo: 2; x = x_hi * 2 + x_lo), y: 4, z: 4, core: 2. Of those that a mesh axis runs over, the one named last changes fastest.
Arguments:
- entities: bfloat16 [131072, 400], P(('blk', 'dom')), may hold values from -1.5 to 1.5
- relations: bfloat16 [16, 400, 400], replicated, may hold values from -0.3125 to 0.3125
- tile_blocks: int32 [1024, 2], P(('blk', 'dom')), may hold values from 0 to 7, all different within a row; in each aligned block of 8 rows (0 to 7, 8 to 15, ...) at most 2 rows name the same one
- src_offset: int32 [1024, 128], P(('blk', 'dom')), may hold values from 0 to 1023
- dst_offset: int32 [1024, 128], P(('blk', 'dom')), may hold values from 0 to 1023
- tile_relation: int32 [1024], P(('blk', 'dom')), may hold values from 0 to 15
- tile_valid: int32 [1024, 128], P(('blk', 'dom')), may hold values from 0 to 1, as said below
- neg_index: int32 [65536], P(('blk', 'dom')), may hold values from 0 to 1023
Outputs:
- edge_loss: float32 [1024, 128], P(('blk', 'dom'))
- positive_grad: float32 [131072, 400], P(('blk', 'dom'))
- negative_grad: float32 [131072, 400], P(('blk', 'dom'))
The draws below stay inside these ranges and needn't reach their ends.
Inputs may be any that keep to these rules, and one draw needn't show every extreme that they name: `tile_valid`: the live slots of each tile are a leading run of at least one slot; the first tile of each device's 8 is full. `tile_blocks`: A tile's two partitions differ; among the 8 tiles of one device, each partition is named at most 2 times over both columns.
All inputs are finite; a program needn't handle non-finite values.
Results may differ from the reference program's by a relative error of at most 0.0031.
Values may be sent and summed in bfloat16 or wider, within the bound.
No kernel may reach another device: no remote copies, remote signals or barrier semaphores. Data moves between devices by JAX's collectives and lax.ppermute only.
A program may use at most 192 MiB of HBM per device.

```python
import math
import jax
import jax.numpy as jnp
import numpy as np
from jax import lax

D = 400
TILE = 128
NREL = 16
ENT_DEV = 1024
NEG_DEV = 512
TILES = 8
ENTITIES = 131072
TILES_ALL = 1024
NEGS = 8192
NEGS_ALL = 65536
CAP = 2
N_BLK = 16
N_DOM = 8


def draw_tile_valid(key, part):
    key = jax.random.fold_in(key, 11)
    level_key, length_key = jax.random.split(key)
    owners = TILES_ALL // TILES
    levels = jax.random.randint(level_key, (owners,), 1, 5)
    tile_ids = jnp.arange(TILES_ALL, dtype=jnp.int32)
    raw = jax.random.randint(length_key, (TILES_ALL,), 0, TILE)
    length = 1 + raw // levels[tile_ids // TILES]
    length = jnp.where(tile_ids % TILES == 0, TILE, length)
    slots = jnp.arange(TILE, dtype=jnp.int32)
    return (slots[None, :] < length[:, None]).astype(jnp.int32)


def set_ends(entries, key, least, largest):
    longest = entries.shape.index(max(entries.shape))
    spots = []
    for shift in (0, 1):
        where = [jax.random.randint(jax.random.fold_in(key, axis), (), 0, length) for axis, length in enumerate(entries.shape)]
        where[longest] = (where[longest] + shift) % entries.shape[longest]
        spots.append(tuple(where))
    return entries.at[spots[0]].set(least).at[spots[1]].set(largest)


def level_of(rng, extent, shards, smallest, top_value):
    level, own = 1.0, jax.random.fold_in(rng, 6)
    for axis_at, blocks in shards:
        draws = jnp.exp(jax.random.uniform(jax.random.fold_in(own, axis_at), (blocks,), jnp.float32, smallest / len(shards), top_value / len(shards)))
        level = level * jnp.repeat(draws, extent[axis_at] // blocks).reshape([-1 if axis == axis_at else 1 for axis in range(len(extent))])
    return level


def routed_block(own_key, own, number, rows, count, top, limit, slope):
    ranking = jax.random.permutation(own_key, count)
    crowded, common = load_shares(count, rows * top, limit, slope, True), load_shares(count, rows * top, limit, slope, False)
    places = jnp.arange(count)

    def named(sizes, turn):
        used = int((sizes > 0).sum())
        fixed = max(1, used // 4)
        moved = fixed + (places - fixed + turn * (used - fixed)) % max(1, count - fixed)
        return jnp.zeros((count,), jnp.int32).at[ranking[jnp.where(places < fixed, places, moved)]].set(jnp.asarray(sizes, jnp.int32))

    sizes = jnp.where(number % 4 == 0, named(crowded, number // 4), named(common, number - number // 4 - 1))
    mixed = jax.random.permutation(jax.random.fold_in(own, 3), count)
    giver, sink = mixed[0:count // 2 * 2:2], mixed[1:count // 2 * 2:2]
    room = jnp.minimum(sizes[giver] - 1, limit - sizes[sink]) // 2
    room = jnp.where((giver == ranking[0]) | (sink == ranking[0]) | (sizes[sink] == 0), 0, jnp.maximum(room, 0))
    moved = jax.random.randint(jax.random.fold_in(own, 4), (count // 2,), 0, 1 << 20) % (room + 1)
    sizes = sizes.at[giver].add(-moved).at[sink].add(moved)
    labels = jnp.searchsorted(jnp.cumsum(sizes), jnp.arange(rows * top), side="right").astype(jnp.int32)
    table = labels.reshape(top, rows).T
    table = table[jax.random.permutation(jax.random.fold_in(own, 1), rows)]
    turn = jax.random.randint(jax.random.fold_in(own, 2), (rows, 1), 0, top)
    return jnp.take_along_axis(table, (jnp.arange(top)[None, :] + turn) % top, axis=1)


def load_shares(amount, total, bound, skew, full):
    loads = [(1 << 20) // math.isqrt(standing ** skew) + 1 for standing in range(1, amount + 1)]
    largest = bound if full else min(bound, max(-(-total // amount), total * loads[0] // sum(loads)))
    least = 1 if total - largest >= amount - 1 else 0
    holding, surplus = [largest] + [least] * (amount - 1), total - largest - least * (amount - 1)
    while surplus > 0:
        free = [i for i in range(1, amount) if holding[i] < largest] or [i for i in range(1, amount) if holding[i] < bound]
        pool, left = sum([loads[i] for i in free]), surplus
        for i in free:
            addition = min(bound - holding[i], max(1, left * loads[i] // pool), surplus)
            holding[i] = holding[i] + addition
            surplus = surplus - addition
    return np.array(holding)


def normal_values(key, shape, width, bound, pieces=(), held_as=jnp.bfloat16):
    entries = jax.random.normal(key, shape, jnp.float32) * width
    if len(pieces) > 0:
        entries = level_of(key, shape, pieces, -0.22, 0.18) * entries
    return jnp.clip(entries, min=-bound, max=bound).astype(held_as)


def setup_inputs(seed: int = 0) -> dict:
    keys = jax.random.split(jax.random.key(seed), 9)
    entities = normal_values(keys[0], (ENTITIES, D), 0.25, 1.5, ((0, 128),))
    relations = normal_values(keys[1], (NREL, D, D), D ** -0.5, 0.3125)
    tile_blocks_keys = jax.random.split(jax.random.fold_in(keys[2], 1), TILES_ALL // TILES)
    tile_blocks_turns = jax.random.permutation(jax.random.fold_in(keys[2], 3), TILES_ALL // TILES)
    tile_blocks = jax.vmap(lambda own, number: routed_block(jax.random.fold_in(keys[2], 2), own, number, TILES, N_DOM, 2, CAP, 0))(tile_blocks_keys, tile_blocks_turns).reshape((TILES_ALL, 2))
    src_offset = set_ends(jax.random.randint(keys[3], (TILES_ALL, TILE), 0, ENT_DEV), jax.random.fold_in(keys[3], 1), 0, ENT_DEV - 1).astype(jnp.int32)
    dst_offset = set_ends(jax.random.randint(keys[4], (TILES_ALL, TILE), 0, ENT_DEV), jax.random.fold_in(keys[4], 1), 0, ENT_DEV - 1).astype(jnp.int32)
    tile_relation = set_ends(jax.random.randint(keys[5], (TILES_ALL,), 0, NREL), jax.random.fold_in(keys[5], 1), 0, NREL - 1).astype(jnp.int32)
    tile_valid = draw_tile_valid(jax.random.fold_in(keys[8], 71), 0)
    neg_index = set_ends(jax.random.randint(keys[7], (NEGS_ALL,), 0, ENT_DEV), jax.random.fold_in(keys[7], 1), 0, ENT_DEV - 1).astype(jnp.int32)
    return {"entities": entities, "relations": relations, "tile_blocks": tile_blocks, "src_offset": src_offset, "dst_offset": dst_offset, "tile_relation": tile_relation, "tile_valid": tile_valid, "neg_index": neg_index}


def reference(entities, relations, tile_blocks, src_offset, dst_offset, tile_relation, tile_valid, neg_index):
    devices = N_BLK * N_DOM
    edges = TILES * TILE
    scale = 1.0 / math.sqrt(NEGS)
    blocks = entities.reshape(devices, ENT_DEV, D)
    owned_neg = neg_index.reshape(devices, NEG_DEV)
    neg_rows = jnp.take_along_axis(blocks, owned_neg[:, :, None], axis=1).reshape(N_BLK, N_DOM, NEG_DEV, D)

    def one_device(device, carry):
        loss_all, pos_all, span_all = carry
        group = device // N_DOM
        column = device % N_DOM
        first = (device * TILES).astype(jnp.int32)
        blocks_here = lax.dynamic_slice_in_dim(tile_blocks, first, TILES, 0)
        src_here = lax.dynamic_slice_in_dim(src_offset, first, TILES, 0)
        dst_here = lax.dynamic_slice_in_dim(dst_offset, first, TILES, 0)
        rel_here = lax.dynamic_slice_in_dim(tile_relation, first, TILES, 0)
        valid_here = lax.dynamic_slice_in_dim(tile_valid, first, TILES, 0)
        base = group * N_DOM * ENT_DEV
        src_index = (base + blocks_here[:, 0:1] * ENT_DEV + src_here).reshape(edges).astype(jnp.int32)
        dst_index = (base + blocks_here[:, 1:2] * ENT_DEV + dst_here).reshape(edges).astype(jnp.int32)
        src_emb = entities[src_index]
        dst_emb = entities[dst_index]
        rel_mats = relations[rel_here].astype(jnp.float32)
        query = jnp.einsum('tpd,tde->tpe', src_emb.reshape(TILES, TILE, D).astype(jnp.float32), rel_mats)
        query = query.astype(jnp.bfloat16).reshape(edges, D)
        positive = lax.optimization_barrier(jnp.sum(query.astype(jnp.float32) * dst_emb.astype(jnp.float32), axis=1)).astype(jnp.bfloat16)
        negs = lax.dynamic_index_in_dim(neg_rows, column, axis=1, keepdims=False).reshape(NEGS, D)
        valid_f = valid_here.reshape(edges).astype(jnp.float32)
        gap = 1.0 + jnp.dot(query, negs.T, preferred_element_type=jnp.float32) - positive.astype(jnp.float32)[:, None]
        loss = valid_f * lax.optimization_barrier(jnp.sum(jax.nn.softplus(gap), axis=1)) / NEGS
        coef = (valid_f[:, None] * jax.nn.sigmoid(gap) * scale).astype(jnp.bfloat16)
        total = lax.optimization_barrier(jnp.sum(coef.astype(jnp.float32), axis=1))
        pulled = jnp.dot(coef, negs, preferred_element_type=jnp.float32)
        query_grad = (pulled - total[:, None] * dst_emb.astype(jnp.float32)).astype(jnp.bfloat16)
        src_term = jnp.einsum('tpe,tde->tpd', query_grad.reshape(TILES, TILE, D).astype(jnp.float32), rel_mats).reshape(edges, D)
        dst_term = -total[:, None] * query.astype(jnp.float32)
        neg_term = jnp.dot(coef.T, query, preferred_element_type=jnp.float32).reshape(N_BLK, NEG_DEV, D)
        loss_all = lax.dynamic_update_slice_in_dim(loss_all, loss.reshape(TILES, TILE), first, 0)
        pos_all = pos_all.at[src_index].add(src_term).at[dst_index].add(dst_term)
        old = lax.dynamic_index_in_dim(span_all, column, axis=1, keepdims=False)
        span_all = lax.dynamic_update_index_in_dim(span_all, old + neg_term, column, 1)
        return (loss_all, pos_all, span_all)
    start = (jnp.zeros((TILES_ALL, TILE), jnp.float32), jnp.zeros((ENTITIES, D), jnp.float32), jnp.zeros((N_BLK, N_DOM, NEG_DEV, D), jnp.float32))
    edge_loss, positive_grad, span_all = lax.fori_loop(jnp.int32(0), jnp.int32(devices), one_device, start)
    rows = (jnp.arange(devices, dtype=jnp.int32)[:, None] * ENT_DEV + owned_neg).reshape(NEGS_ALL)
    negative_grad = jnp.zeros((ENTITIES, D), jnp.float32).at[rows].add(span_all.reshape(NEGS_ALL, D))
    return (edge_loss, positive_grad, negative_grad)
```

```python
import functools
import math

import jax
import jax.numpy as jnp
from jax import lax
from jax.experimental import pallas as pl
from jax.experimental.pallas import tpu as pltpu
from jax.sharding import PartitionSpec as P

BF = jnp.bfloat16
F32 = jnp.float32
LOG2E = math.log2(math.e)
LANES = 128
EXTRA = 16
NT = (((1,), (1,)), ((), ()))


def whole(count):
    return [pl.BlockSpec(memory_space=pltpu.VMEM)] * count


def one_hot(rows, index_row):
    place = lax.broadcasted_iota(jnp.int32, (rows, index_row.shape[1]), 0)
    return jnp.where(place == index_row, 1.0, 0.0).astype(BF)


def turn_kernel(ent_ref, neg_ref, turned_ref, own_ref):
    rows, width = ent_ref.shape
    turned = ent_ref[...].astype(F32).T.astype(BF)
    turned_ref[...] = turned
    picked = jnp.dot(turned, one_hot(rows, neg_ref[...]), preferred_element_type=F32)
    own_ref[:width, :] = picked.astype(BF)
    line = lax.broadcasted_iota(jnp.int32, (EXTRA, own_ref.shape[1]), 0)
    own_ref[width:, :] = jnp.where(line < 2, 1.0, 0.0).astype(BF)


def pick_kernel(turned_ref, need_ref, send_ref):
    rows = turned_ref.shape[1]
    hot = one_hot(rows, need_ref[0])
    send_ref[0] = jnp.dot(turned_ref[...], hot, preferred_element_type=F32).astype(BF)


def end_block(ref, slot):
    return ref[slot // 2, :, pl.ds(pl.multiple_of(slot % 2 * LANES, LANES), LANES)]


def query_kernel(scale, rel_id, slots, rel_ref, recv_ref, valid_ref, query_ref, turned_ref, weight_ref):
    t = pl.program_id(0)
    width = rel_ref.shape[1]
    src = end_block(recv_ref, slots[2 * t]).astype(F32).T.astype(BF)
    dst = end_block(recv_ref, slots[2 * t + 1]).astype(F32)
    query = jnp.dot(src, rel_ref[0], preferred_element_type=F32).astype(BF).astype(F32).T
    positive = jnp.sum(query * dst, axis=0, keepdims=True).astype(BF).astype(F32)
    turned_ref[...] = query.astype(BF)
    line = lax.broadcasted_iota(jnp.int32, (EXTRA, LANES), 0)
    extra = jnp.where(line == 0, -positive, jnp.where(line == 1, 1.0, 0.0))
    rest = jnp.zeros((query_ref.shape[1] - width - EXTRA, LANES), F32)
    query_ref[...] = jnp.concatenate([query, extra, rest], axis=0).T.astype(BF)
    weight = valid_ref[0].astype(F32) * scale
    weight_ref[...] = jnp.broadcast_to(weight, (LANES, LANES)).T


def weigh(gap, coef_ref, rows, grow_ref, ramp_ref, weight_ref):
    grow, ramp, weight = grow_ref[rows, :], ramp_ref[rows, :], weight_ref[rows, :]
    for k in range(gap.shape[1] // LANES):
        x = gap[:, k * LANES : (k + 1) * LANES]
        e = jnp.exp2(jnp.abs(x) * (-LOG2E))
        d = 1.0 + e
        coef = jnp.where(x >= 0, 1.0, e) / d * weight
        coef_ref[rows, k * LANES : (k + 1) * LANES] = coef.astype(BF)
        ramp = ramp + jnp.maximum(x, 0.0)
        grow = grow * d + e
    grow_ref[rows, :] = grow
    ramp_ref[rows, :] = ramp


def score_kernel(first, step, *refs):
    query_ref, turned_ref, weight_ref = refs[:3]
    count = 8
    negs = refs[3 : 3 + count]
    rest = refs[3 + count :]
    if first:
        pulled_in = None
    else:
        pulled_in, grow_in, ramp_in = rest[:3]
        rest = rest[3:]
    pulled_ref, grow_ref, ramp_ref, swap_ref = rest[:4]
    kept = rest[4:8]
    coefs = rest[8:10]
    edges = query_ref.shape[0]
    wide = negs[0].shape[0]
    span = negs[0].shape[1]
    blocks = edges // step
    if first:
        pulled_ref[...] = jnp.zeros_like(pulled_ref)
        grow_ref[...] = jnp.zeros_like(grow_ref)
        ramp_ref[...] = jnp.zeros_like(ramp_ref)
    else:
        pulled_ref[...] = pulled_in[...]
        grow_ref[...] = grow_in[...]
        ramp_ref[...] = ramp_in[...]

    def score(r, b):
        return jnp.dot(query_ref[b * step : (b + 1) * step, :wide], negs[r][...], preferred_element_type=F32)

    def pull(r, b):
        at = slice(b * step, (b + 1) * step)
        pulled_ref[:, at] += lax.dot_general(negs[r][...], coefs[r % 2][at, :], NT, preferred_element_type=F32)

    def push(r, half):
        at = slice(half * span // 2, (half + 1) * span // 2)
        term = jnp.dot(turned_ref[...], coefs[r % 2][:, at], preferred_element_type=F32)
        if r < 4:
            swap_ref[r, :, at] = term.astype(BF)
        else:
            kept[r - 4][:, at] = term

    units = [(r, b) for r in range(count) for b in range(blocks)]
    gap = score(*units[0])
    for i, (r, b) in enumerate(units):
        after = score(*units[i + 1]) if i + 1 < len(units) else None
        weigh(gap, coefs[r % 2], pl.ds(b * step, step), grow_ref, ramp_ref, weight_ref)
        if r > 0:
            pull(r - 1, b)
            if b % (blocks // 2) == blocks // 2 - 1:
                push(r - 1, b // (blocks // 2))
        gap = after
    for b in range(blocks):
        pull(count - 1, b)
    push(count - 1, 0)
    push(count - 1, 1)


def score_call(query, turned, weight, negs, carry):
    edges = query.shape[0]
    wide, span = negs[0].shape
    width = turned.shape[0]
    first = carry is None
    ins = [query, turned, weight, *negs] + ([] if first else list(carry))
    outs = (
        jax.ShapeDtypeStruct((wide, edges), F32),
        jax.ShapeDtypeStruct((edges, LANES), F32),
        jax.ShapeDtypeStruct((edges, LANES), F32),
        jax.ShapeDtypeStruct((4, width, span), BF),
    ) + (jax.ShapeDtypeStruct((width, span), F32),) * 4
    got = pl.pallas_call(
        functools.partial(score_kernel, first, 256),
        out_shape=outs,
        in_specs=whole(len(ins)),
        out_specs=tuple(whole(len(outs))),
        scratch_shapes=[pltpu.VMEM((edges, span), BF)] * 2,
        compiler_params=pltpu.CompilerParams(vmem_limit_bytes=50 << 20),
        cost_estimate=pl.CostEstimate(
            flops=6 * edges * 8 * span * width, bytes_accessed=16 << 20, transcendentals=0
        ),
    )(*ins)
    return got[:3], got[3], got[4:]


def back_kernel(rel_id, slots, rel_ref, recv_ref, pulled_ref, turned_ref, send_ref):
    t = pl.program_id(0)
    width = rel_ref.shape[1]
    dst = end_block(recv_ref, slots[2 * t + 1]).astype(F32)
    total = pulled_ref[width : width + 1, :]
    grad = (pulled_ref[:width, :] - total * dst).astype(BF)
    src_term = jnp.dot(rel_ref[0], grad, preferred_element_type=F32)
    dst_term = -total * turned_ref[...].astype(F32)
    for end, term in ((0, src_term), (1, dst_term)):
        slot = slots[2 * t + end]
        at = pl.ds(pl.multiple_of(slot % 2 * LANES, LANES), LANES)
        send_ref[slot // 2, :, at] = term.astype(BF)


def place_kernel(need_ref, term_ref, out_ref):
    @pl.when(pl.program_id(0) == 0)
    def _():
        out_ref[...] = jnp.zeros_like(out_ref)

    hot = one_hot(out_ref.shape[0], need_ref[0])
    out_ref[...] += lax.dot_general(hot, term_ref[0], NT, preferred_element_type=F32)


def span_kernel(neg_ref, *refs):
    out_ref = refs[-1]
    total = refs[0][...].astype(F32)
    for ref in refs[1:-1]:
        total = total + ref[...].astype(F32)
    high = total.astype(BF)
    low = (total - high.astype(F32)).astype(BF)
    hot = one_hot(out_ref.shape[0], neg_ref[...])
    out_ref[...] = lax.dot_general(hot, high, NT, preferred_element_type=F32) + lax.dot_general(
        hot, low, NT, preferred_element_type=F32
    )


def across_z(value, shift):
    pairs = []
    for i in range(16):
        z = (i >> 1) & 3
        pairs.append((i, (i & 9) | (((z + shift) % 4) << 1)))
    return lax.ppermute(value, "blk", pairs)


def across_x(value):
    return lax.ppermute(value, "blk", [(i, i ^ 8) for i in range(16)])


def across_core(value):
    return lax.ppermute(value, "blk", [(i, i ^ 1) for i in range(16)])


def on_device(
    entities, relations, tile_blocks, src_offset, dst_offset, tile_relation, tile_valid, neg_index
):
    ent_dev, width = entities.shape
    tiles, tile = src_offset.shape
    edges = tiles * tile
    ends = 2 * tiles
    doms = lax.axis_size("dom")
    span = neg_index.shape[0]
    negs_count = span * lax.axis_size("blk")
    wide = width + EXTRA
    params = pltpu.CompilerParams(vmem_limit_bytes=40 << 20)

    named = tile_blocks.reshape(ends)
    order = jnp.arange(ends)
    earlier = (named[None, :] == named[:, None]) & (order[None, :] < order[:, None])
    slots = 2 * named + jnp.sum(earlier.astype(jnp.int32), axis=1)
    offsets = jnp.stack([src_offset, dst_offset], axis=1).reshape(ends, tile)
    chosen = slots[None, :] == order[:, None]
    wanted = jnp.sum(jnp.where(chosen[:, :, None], offsets[None], 0), axis=1)
    need = lax.all_to_all(wanted.reshape(doms, 1, 2 * tile), "dom", 0, 0)

    neg_row = neg_index.reshape(1, span)
    turned_ent, own = pl.pallas_call(
        turn_kernel,
        out_shape=(
            jax.ShapeDtypeStruct((width, ent_dev), BF),
            jax.ShapeDtypeStruct((wide, span), BF),
        ),
        in_specs=whole(2),
        out_specs=tuple(whole(2)),
        compiler_params=params,
    )(entities, neg_row)

    near = [[None, None], [None, None]]
    side = across_x(own)
    for h, base in ((0, own), (1, side)):
        near[h][0] = [base] + [across_z(base, -r) for r in (1, 2, 3)]
        near[h][1] = [across_core(value) for value in near[h][0]]

    send = pl.pallas_call(
        pick_kernel,
        grid=(doms,),
        out_shape=jax.ShapeDtypeStruct((doms, width, 2 * tile), BF),
        in_specs=[
            pl.BlockSpec((width, ent_dev), lambda g: (0, 0)),
            pl.BlockSpec((1, 1, 2 * tile), lambda g: (g, 0, 0)),
        ],
        out_specs=pl.BlockSpec((1, width, 2 * tile), lambda g: (g, 0, 0)),
        compiler_params=params,
    )(turned_ent, need)
    recv = lax.all_to_all(send, "dom", 0, 0)

    query, turned, weight = pl.pallas_call(
        functools.partial(query_kernel, 1.0 / math.sqrt(negs_count)),
        out_shape=(
            jax.ShapeDtypeStruct((edges, 4 * LANES), BF),
            jax.ShapeDtypeStruct((width, edges), BF),
            jax.ShapeDtypeStruct((edges, LANES), F32),
        ),
        grid_spec=pltpu.PrefetchScalarGridSpec(
            num_scalar_prefetch=2,
            grid=(tiles,),
            in_specs=[
                pl.BlockSpec((1, width, width), lambda t, rel, slot: (rel[t], 0, 0)),
                pl.BlockSpec((doms, width, 2 * tile), lambda t, rel, slot: (0, 0, 0)),
                pl.BlockSpec((1, 1, tile), lambda t, rel, slot: (t, 0, 0)),
            ],
            out_specs=(
                pl.BlockSpec((tile, 4 * LANES), lambda t, rel, slot: (t, 0)),
                pl.BlockSpec((width, tile), lambda t, rel, slot: (0, t)),
                pl.BlockSpec((tile, LANES), lambda t, rel, slot: (t, 0)),
            ),
        ),
        compiler_params=params,
    )(tile_relation, slots, relations, recv, tile_valid.reshape(tiles, 1, tile))

    carry, far_swap, far_kept = score_call(query, turned, weight, near[1][1] + near[1][0], None)
    far_swapped = across_core(far_swap)
    far = [(far_kept[r] + far_swapped[r].astype(F32)).astype(BF) for r in range(4)]
    far_sum = far[0].astype(F32)
    for r in (1, 2, 3):
        far_sum = far_sum + across_z(far[r], r).astype(F32)
    from_side = across_x(far_sum.astype(BF))

    carry, swap, kept = score_call(query, turned, weight, near[0][1] + near[0][0], carry)
    pulled, grow, ramp = carry
    swapped = across_core(swap)
    mine = [(kept[r] + swapped[r].astype(F32)).astype(BF) for r in range(4)]
    parts = [mine[0]] + [across_z(mine[r], r) for r in (1, 2, 3)] + [from_side]

    terms = pl.pallas_call(
        back_kernel,
        out_shape=jax.ShapeDtypeStruct((doms, width, 2 * tile), BF),
        grid_spec=pltpu.PrefetchScalarGridSpec(
            num_scalar_prefetch=2,
            grid=(tiles,),
            in_specs=[
                pl.BlockSpec((1, width, width), lambda t, rel, slot: (rel[t], 0, 0)),
                pl.BlockSpec((doms, width, 2 * tile), lambda t, rel, slot: (0, 0, 0)),
                pl.BlockSpec((wide, tile), lambda t, rel, slot: (0, t)),
                pl.BlockSpec((width, tile), lambda t, rel, slot: (0, t)),
            ],
            out_specs=pl.BlockSpec((doms, width, 2 * tile), lambda t, rel, slot: (0, 0, 0)),
        ),
        compiler_params=params,
    )(tile_relation, slots, relations, recv, pulled, turned)
    back = lax.all_to_all(terms, "dom", 0, 0)

    positive_grad = pl.pallas_call(
        place_kernel,
        grid=(doms,),
        out_shape=jax.ShapeDtypeStruct((ent_dev, width), F32),
        in_specs=[
            pl.BlockSpec((1, 1, 2 * tile), lambda g: (g, 0, 0)),
            pl.BlockSpec((1, width, 2 * tile), lambda g: (g, 0, 0)),
        ],
        out_specs=pl.BlockSpec((ent_dev, width), lambda g: (0, 0)),
        compiler_params=params,
    )(need, back)

    negative_grad = pl.pallas_call(
        span_kernel,
        out_shape=jax.ShapeDtypeStruct((ent_dev, width), F32),
        in_specs=whole(1 + len(parts)),
        out_specs=whole(1)[0],
        compiler_params=params,
    )(neg_row, *parts)

    loss = jnp.sum(jnp.log1p(grow) + ramp, axis=1).reshape(tiles, tile) / negs_count
    edge_loss = tile_valid.astype(F32) * loss
    return (edge_loss, positive_grad, negative_grad)


def solution(mesh):
    placed = (
        P(("blk", "dom"), None),
        P(),
        P(("blk", "dom"), None),
        P(("blk", "dom"), None),
        P(("blk", "dom"), None),
        P(("blk", "dom")),
        P(("blk", "dom"), None),
        P(("blk", "dom")),
    )
    return jax.shard_map(
        on_device,
        mesh=mesh,
        in_specs=placed,
        out_specs=(P(("blk", "dom"), None), P(("blk", "dom"), None), P(("blk", "dom"), None)),
        check_vma=False,
    )
```

```python
import functools
import math

import jax
import jax.numpy as jnp
from jax import lax
from jax.experimental import pallas as pl
from jax.experimental.pallas import tpu as pltpu
from jax.sharding import PartitionSpec as P

BF = jnp.bfloat16
F32 = jnp.float32
LOG2E = math.log2(math.e)
LANES = 128
VMEM_LIMIT = 18 << 20
K3_LIMIT = 40 << 20
K2_FLOPS = 1 << 33
EXTRA = 16
NT = (((1,), (1,)), ((), ()))


def whole(count):
    return [pl.BlockSpec(memory_space=pltpu.VMEM)] * count


def one_hot(rows, index_row):
    place = lax.broadcasted_iota(jnp.int32, (rows, index_row.shape[1]), 0)
    return jnp.where(place == index_row, 1.0, 0.0).astype(BF)


def own_kernel(ent_ref, neg_ref, own_ref):
    width, rows = ent_ref.shape
    picked = jnp.dot(ent_ref[...], one_hot(rows, neg_ref[...]), preferred_element_type=F32)
    own_ref[:width, :] = picked.astype(BF)
    line = lax.broadcasted_iota(jnp.int32, (EXTRA, own_ref.shape[1]), 0)
    own_ref[width:, :] = jnp.where(line < 2, 1.0, 0.0).astype(BF)


def pick_kernel(turned_ref, need_ref, send_ref):
    rows = turned_ref.shape[1]
    for g in range(need_ref.shape[0]):
        hot = one_hot(rows, need_ref[g])
        send_ref[g] = jnp.dot(turned_ref[...], hot, preferred_element_type=F32).astype(BF)


def end_block(ref, slot):
    return ref[slot // 2, :, pl.ds(pl.multiple_of(slot % 2 * LANES, LANES), LANES)]


def query_kernel(scale, rel_id, slots, rel_ref, recv_ref, valid_ref, pair_ref, query_ref, turned_ref, *refs):
    weight_refs, own_ref, sems = refs[:2], refs[2], refs[3]
    tiles, width = own_ref.shape[:2]
    loads = [pltpu.make_async_copy(rel_ref.at[rel_id[t]], own_ref.at[t], sems.at[t]) for t in range(tiles)]
    for load in loads:
        load.start()
    for live_ref, weight_ref in zip((valid_ref, pair_ref), weight_refs):
        weight = live_ref[...] * scale
        for t in range(tiles):
            at = slice(t * LANES, (t + 1) * LANES)
            weight_ref[at, :] = jnp.broadcast_to(weight[t : t + 1, :], (LANES, LANES)).T
    sources = [end_block(recv_ref, slots[2 * t]).astype(F32).T.astype(BF) for t in range(tiles)]
    for load in loads:
        load.wait()
    line = lax.broadcasted_iota(jnp.int32, (EXTRA, LANES), 0)
    rest = jnp.zeros((query_ref.shape[1] - width - EXTRA, LANES), F32)
    for t in range(tiles):
        at = slice(t * LANES, (t + 1) * LANES)
        dst = end_block(recv_ref, slots[2 * t + 1]).astype(F32)
        query = jnp.dot(sources[t], own_ref[t], preferred_element_type=F32).astype(BF).astype(F32).T
        positive = jnp.sum(query * dst, axis=0, keepdims=True).astype(BF).astype(F32)
        turned_ref[:, at] = query.astype(BF)
        extra = jnp.where(line == 0, -positive, jnp.where(line == 1, 1.0, 0.0))
        query_ref[at, :] = jnp.concatenate([query, extra, rest], axis=0).T.astype(BF)


def weigh(gap, coef_ref, rows, grow_ref, ramp_ref, weight_ref):
    grow, ramp, weight = grow_ref[rows, :], ramp_ref[rows, :], weight_ref[rows, :]
    for k in range(gap.shape[1] // LANES):
        x = gap[:, k * LANES : (k + 1) * LANES]
        e = jnp.exp2(jnp.abs(x) * (-LOG2E))
        d = 1.0 + e
        coef = jnp.where(x >= 0, 1.0, e) / d * weight
        coef_ref[rows, k * LANES : (k + 1) * LANES] = coef.astype(BF)
        ramp = ramp + jnp.maximum(x, 0.0)
        grow = grow * d + e
    grow_ref[rows, :] = grow
    ramp_ref[rows, :] = ramp


def score_kernel(first, base, split, count, step, *refs):
    query_ref, turned_ref, weight_ref = refs[:3]
    negs = refs[3 : 3 + count]
    rest = refs[3 + count :]
    if not first:
        pulled_in, grow_in, ramp_in = rest[:3]
        rest = rest[3:]
    if base:
        base_ref, rest = rest[0], rest[1:]
    pulled_ref, grow_ref, ramp_ref = rest[:3]
    if split:
        terms, rest = rest[3 : 3 + count], rest[3 + count :]
    else:
        terms, rest = [rest[3].at[r] for r in range(count)], rest[4:]
    coefs = rest
    edges = query_ref.shape[0]
    wide, span = negs[0].shape
    blocks = edges // step
    if first:
        pulled_ref[...] = jnp.zeros_like(pulled_ref)
        grow_ref[...] = jnp.zeros_like(grow_ref)
        ramp_ref[...] = jnp.zeros_like(ramp_ref)
    else:
        pulled_ref[...] = pulled_in[...]
        grow_ref[...] = grow_in[...]
        ramp_ref[...] = ramp_in[...]

    def score(r, b):
        return jnp.dot(query_ref[b * step : (b + 1) * step, :wide], negs[r][...], preferred_element_type=F32)

    def pull(r, b):
        at = slice(b * step, (b + 1) * step)
        pulled_ref[:, at] += lax.dot_general(negs[r][...], coefs[r % 2][at, :], NT, preferred_element_type=F32)

    def push(r, half):
        at = slice(half * span // 2, (half + 1) * span // 2)
        term = jnp.dot(turned_ref[...], coefs[r % 2][:, at], preferred_element_type=F32)
        if base:
            term = term + base_ref[r, :, at].astype(F32)
        terms[r][:, at] = term.astype(terms[r].dtype)

    units = [(r, b) for r in range(count) for b in range(blocks)]
    gap = score(*units[0])
    for i, (r, b) in enumerate(units):
        after = score(*units[i + 1]) if i + 1 < len(units) else None
        weigh(gap, coefs[r % 2], pl.ds(b * step, step), grow_ref, ramp_ref, weight_ref)
        if r > 0:
            pull(r - 1, b)
            if b % (blocks // 2) == blocks // 2 - 1:
                push(r - 1, b // (blocks // 2))
        gap = after
    for b in range(blocks):
        pull(count - 1, b)
    push(count - 1, 0)
    push(count - 1, 1)


def score_call(query, turned, weight, negs, carry, base, split):
    edges = query.shape[0]
    wide, span = negs[0].shape
    width = turned.shape[0]
    count = len(negs)
    first = carry is None
    ins = [query, turned, weight, *negs] + ([] if first else list(carry)) + ([] if base is None else [base])
    outs = (
        jax.ShapeDtypeStruct((wide, edges), F32),
        jax.ShapeDtypeStruct((edges, LANES), F32),
        jax.ShapeDtypeStruct((edges, LANES), F32),
    )
    if split:
        outs += (jax.ShapeDtypeStruct((width, span), BF),) * count
    else:
        outs += (jax.ShapeDtypeStruct((count, width, span), F32),)
    got = pl.pallas_call(
        functools.partial(score_kernel, first, base is not None, split, count, 256),
        out_shape=outs,
        in_specs=whole(len(ins)),
        out_specs=tuple(whole(len(outs))),
        scratch_shapes=[pltpu.VMEM((edges, span), BF)] * 2,
        compiler_params=pltpu.CompilerParams(vmem_limit_bytes=VMEM_LIMIT),
        cost_estimate=pl.CostEstimate(flops=1, bytes_accessed=1, transcendentals=0),
    )(*ins)
    return got[:3], got[3:] if split else got[3]


def back_kernel(slots, rel_ref, recv_ref, pulled_ref, turned_ref, *refs):
    pair_ref, far_0, far_1, far_2, far_3, near_2, send_ref, side_ref, joined_ref = refs
    side_ref[...] = (far_0[...].astype(F32) + far_1[...].astype(F32) + far_3[...].astype(F32)).astype(BF)
    joined_ref[...] = (near_2[...].astype(F32) + far_2[...].astype(F32)).astype(BF)
    tiles, width = rel_ref.shape[:2]
    for t in range(tiles):
        at = slice(t * LANES, (t + 1) * LANES)
        dst = end_block(recv_ref, slots[2 * t + 1]).astype(F32)
        pulled = pulled_ref[:, at] + pair_ref[:, at]
        total = pulled[width : width + 1]
        grad = (pulled[:width] - total * dst).astype(BF)
        src_term = jnp.dot(rel_ref[t], grad, preferred_element_type=F32)
        dst_term = -total * turned_ref[:, at].astype(F32)
        for end, term in ((0, src_term), (1, dst_term)):
            slot = slots[2 * t + end]
            there = pl.ds(pl.multiple_of(slot % 2 * LANES, LANES), LANES)
            send_ref[slot // 2, :, there] = term.astype(BF)


def place_kernel(need_ref, term_ref, out_ref):
    rows = out_ref.shape[1]
    total = jnp.zeros(out_ref.shape, F32)
    for g in range(need_ref.shape[0]):
        total = total + lax.dot_general(term_ref[g], one_hot(rows, need_ref[g]), NT, preferred_element_type=F32)
    out_ref[...] = total


def span_kernel(neg_ref, *refs):
    out_ref = refs[-1]
    total = refs[0][...].astype(F32)
    for ref in refs[1:-1]:
        total = total + ref[...].astype(F32)
    high = total.astype(BF)
    low = (total - high.astype(F32)).astype(BF)
    hot = one_hot(out_ref.shape[1], neg_ref[...])
    out_ref[...] = lax.dot_general(high, hot, NT, preferred_element_type=F32) + lax.dot_general(
        low, hot, NT, preferred_element_type=F32
    )


def across_z(value, shift):
    pairs = []
    for i in range(16):
        z = (i >> 1) & 3
        pairs.append((i, (i & 9) | (((z + shift) % 4) << 1)))
    return lax.ppermute(value, "blk", pairs)


def across_x(value):
    return lax.ppermute(value, "blk", [(i, i ^ 8) for i in range(16)])


def across_core(value):
    return lax.ppermute(value, "blk", [(i, i ^ 1) for i in range(16)])


def on_device(
    entities, relations, tile_blocks, src_offset, dst_offset, tile_relation, tile_valid, neg_index
):
    ent_dev, width = entities.shape
    tiles, tile = src_offset.shape
    edges = tiles * tile
    ends = 2 * tiles
    doms = lax.axis_size("dom")
    span = neg_index.shape[0]
    negs_count = span * lax.axis_size("blk")
    wide = width + EXTRA
    params = pltpu.CompilerParams(vmem_limit_bytes=8 << 20)
    wide_params = pltpu.CompilerParams(vmem_limit_bytes=14 << 20)

    named = tile_blocks.reshape(ends)
    order = jnp.arange(ends)
    earlier = (named[None, :] == named[:, None]) & (order[None, :] < order[:, None])
    slots = 2 * named + jnp.sum(earlier.astype(jnp.int32), axis=1)
    offsets = jnp.stack([src_offset, dst_offset], axis=1).reshape(ends, tile)
    chosen = slots[None, :] == order[:, None]
    wanted = jnp.sum(jnp.where(chosen[:, :, None], offsets[None], 0), axis=1)
    need = lax.all_to_all(wanted.reshape(doms, 1, 2 * tile), "dom", 0, 0)

    wanted, neg_index = lax.optimization_barrier((wanted, neg_index))
    live = tile_valid.astype(F32)
    pair_live = across_core(live)
    neg_row = neg_index.reshape(1, span)
    turned_ent = entities.T
    own = pl.pallas_call(
        own_kernel,
        out_shape=jax.ShapeDtypeStruct((wide, span), BF),
        in_specs=whole(2),
        out_specs=whole(1)[0],
        compiler_params=params,
    )(turned_ent, neg_row)

    side = across_x(own)
    near = [own] + [across_z(own, -r) for r in (1, 2, 3)]

    in_smem = pl.BlockSpec(memory_space=pltpu.SMEM)
    send = pl.pallas_call(
        pick_kernel,
        out_shape=jax.ShapeDtypeStruct((doms, width, 2 * tile), BF),
        in_specs=whole(2),
        out_specs=whole(1)[0],
        compiler_params=params,
        cost_estimate=pl.CostEstimate(flops=K2_FLOPS, bytes_accessed=1 << 23, transcendentals=0),
    )(turned_ent, need)
    send, side, near[2] = lax.optimization_barrier((send, side, near[2]))
    recv = lax.all_to_all(send, "dom", 0, 0)
    far = [side, across_z(side, -1), across_x(near[2]), across_z(side, -3)]
    recv, near[1], near[3], *far[1:] = lax.optimization_barrier((recv, near[1], near[3], *far[1:]))
    query, turned, weight, pair_weight, own_rels = pl.pallas_call(
        functools.partial(query_kernel, 1.0 / math.sqrt(negs_count)),
        out_shape=(
            jax.ShapeDtypeStruct((edges, 4 * LANES), BF),
            jax.ShapeDtypeStruct((width, edges), BF),
            jax.ShapeDtypeStruct((edges, LANES), F32),
            jax.ShapeDtypeStruct((edges, LANES), F32),
            jax.ShapeDtypeStruct((tiles, width, width), BF),
        ),
        in_specs=[in_smem, in_smem, pl.BlockSpec(memory_space=pl.ANY)] + whole(3),
        out_specs=tuple(whole(5)),
        scratch_shapes=[pltpu.SemaphoreType.DMA((tiles,))],
        compiler_params=pltpu.CompilerParams(vmem_limit_bytes=K3_LIMIT),
        cost_estimate=pl.CostEstimate(flops=1, bytes_accessed=1, transcendentals=0),
    )(tile_relation, slots, relations, recv, live, pair_live)

    pair_query, pair_turned = across_core(query), across_core(turned)
    carry, far_terms = score_call(query, turned, weight, far, None, None, False)
    pair_carry, far_sums = score_call(pair_query, pair_turned, pair_weight, far, None, far_terms, True)
    far_1, far_2, far_3 = across_z(far_sums[1], 1), across_x(far_sums[2]), across_z(far_sums[3], 3)
    pair_carry, near_terms = score_call(pair_query, pair_turned, pair_weight, near, pair_carry, None, False)
    pair_pulled = across_core(pair_carry[0])
    pair_loss = across_core(jnp.sum(jnp.log1p(pair_carry[1]) + pair_carry[2], axis=1).reshape(tiles, tile))
    carry, near_sums = score_call(query, turned, weight, near, carry, near_terms, True)
    pulled, grow, ramp = carry
    terms, side_sum, joined = pl.pallas_call(
        back_kernel,
        out_shape=(jax.ShapeDtypeStruct((doms, width, 2 * tile), BF),)
        + (jax.ShapeDtypeStruct((width, span), BF),) * 2,
        in_specs=[in_smem] + whole(10),
        out_specs=tuple(whole(3)),
        compiler_params=wide_params,
    )(slots, own_rels, recv, pulled, turned, pair_pulled, far_sums[0], far_1, far_2, far_3, near_sums[2])
    back = lax.all_to_all(terms, "dom", 0, 0)
    from_side = across_x(side_sum)
    parts = [from_side, near_sums[0], across_z(joined, 2), across_z(near_sums[1], 1), across_z(near_sums[3], 3)]

    positive_grad = pl.pallas_call(
        place_kernel,
        out_shape=jax.ShapeDtypeStruct((width, ent_dev), F32),
        in_specs=whole(2),
        out_specs=whole(1)[0],
        compiler_params=params,
    )(need, back)

    positive_grad, *parts = lax.optimization_barrier((positive_grad, *parts))
    negative_grad = pl.pallas_call(
        span_kernel,
        out_shape=jax.ShapeDtypeStruct((width, ent_dev), F32),
        in_specs=whole(1 + len(parts)),
        out_specs=whole(1)[0],
        compiler_params=params,
    )(neg_row, *parts)

    loss = jnp.sum(jnp.log1p(grow) + ramp, axis=1).reshape(tiles, tile) + pair_loss
    edge_loss = live * (loss / negs_count)
    return (edge_loss, positive_grad.T, negative_grad.T)


def solution(mesh):
    placed = (
        P(("blk", "dom"), None),
        P(),
        P(("blk", "dom"), None),
        P(("blk", "dom"), None),
        P(("blk", "dom"), None),
        P(("blk", "dom")),
        P(("blk", "dom"), None),
        P(("blk", "dom")),
    )
    return jax.shard_map(
        on_device,
        mesh=mesh,
        in_specs=placed,
        out_specs=(P(("blk", "dom"), None), P(("blk", "dom"), None), P(("blk", "dom"), None)),
        check_vma=False,
    )
```

```python
import functools
import math

import jax
import jax.numpy as jnp
from jax import lax
from jax.experimental import pallas as pl
from jax.experimental.pallas import tpu as pltpu
from jax.sharding import PartitionSpec as P

BF = jnp.bfloat16
F32 = jnp.float32
LOG2E = math.log2(math.e)
LANES = 128
VMEM_LIMIT = 18 << 20
K3_LIMIT = 46 << 20
K2_FLOPS = 1 << 33
EXTRA = 16
NT = (((1,), (1,)), ((), ()))


def whole(count):
    return [pl.BlockSpec(memory_space=pltpu.VMEM)] * count


def one_hot(rows, index_row):
    place = lax.broadcasted_iota(jnp.int32, (rows, index_row.shape[1]), 0)
    return jnp.where(place == index_row, 1.0, 0.0).astype(BF)


def own_kernel(ent_ref, neg_ref, own_ref):
    width, rows = ent_ref.shape
    picked = jnp.dot(ent_ref[...], one_hot(rows, neg_ref[...]), preferred_element_type=F32)
    own_ref[:width, :] = picked.astype(BF)
    line = lax.broadcasted_iota(jnp.int32, (EXTRA, own_ref.shape[1]), 0)
    own_ref[width:, :] = jnp.where(line < 2, 1.0, 0.0).astype(BF)


def pick_kernel(turned_ref, need_ref, send_ref):
    rows = turned_ref.shape[1]
    for g in range(need_ref.shape[0]):
        hot = one_hot(rows, need_ref[g])
        send_ref[g] = jnp.dot(turned_ref[...], hot, preferred_element_type=F32).astype(BF)


def end_block(ref, slot):
    return ref[slot // 2, :, pl.ds(pl.multiple_of(slot % 2 * LANES, LANES), LANES)]


def query_kernel(scale, rel_id, slots, rel_ref, recv_ref, valid_ref, pair_ref, query_ref, turned_ref, *refs):
    weight_refs, own_ref, sems = refs[:2], refs[2], refs[3]
    tiles, width = own_ref.shape[:2]
    loads = [pltpu.make_async_copy(rel_ref.at[rel_id[t]], own_ref.at[t], sems.at[t]) for t in range(tiles)]
    for load in loads:
        load.start()
    for live_ref, weight_ref in zip((valid_ref, pair_ref), weight_refs):
        weight = live_ref[...] * scale
        for t in range(tiles):
            at = slice(t * LANES, (t + 1) * LANES)
            weight_ref[at, :] = jnp.broadcast_to(weight[t : t + 1, :], (LANES, LANES)).T
    sources = [end_block(recv_ref, slots[2 * t]).astype(F32).T.astype(BF) for t in range(tiles)]
    for load in loads:
        load.wait()
    line = lax.broadcasted_iota(jnp.int32, (EXTRA, LANES), 0)
    rest = jnp.zeros((query_ref.shape[1] - width - EXTRA, LANES), F32)
    for t in range(tiles):
        at = slice(t * LANES, (t + 1) * LANES)
        dst = end_block(recv_ref, slots[2 * t + 1]).astype(F32)
        query = jnp.dot(sources[t], own_ref[t], preferred_element_type=F32).astype(BF).astype(F32).T
        positive = jnp.sum(query * dst, axis=0, keepdims=True).astype(BF).astype(F32)
        turned_ref[:, at] = query.astype(BF)
        extra = jnp.where(line == 0, -positive, jnp.where(line == 1, 1.0, 0.0))
        query_ref[at, :] = jnp.concatenate([query, extra, rest], axis=0).T.astype(BF)


def weigh(gap, coef_ref, rows, grow_ref, ramp_ref, weight_ref):
    grow, ramp, weight = grow_ref[rows, :], ramp_ref[rows, :], weight_ref[rows, :]
    for k in range(gap.shape[1] // LANES):
        x = gap[:, k * LANES : (k + 1) * LANES]
        e = jnp.exp2(jnp.abs(x) * (-LOG2E))
        d = 1.0 + e
        coef = jnp.where(x >= 0, 1.0, e) / d * weight
        coef_ref[rows, k * LANES : (k + 1) * LANES] = coef.astype(BF)
        ramp = ramp + jnp.maximum(x, 0.0)
        grow = grow * d + e
    grow_ref[rows, :] = grow
    ramp_ref[rows, :] = ramp


def score_kernel(first, base, split, count, step, *refs):
    query_ref, turned_ref, weight_ref = refs[:3]
    negs = refs[3 : 3 + count]
    rest = refs[3 + count :]
    if not first:
        pulled_in, grow_in, ramp_in = rest[:3]
        rest = rest[3:]
    if base:
        base_ref, rest = rest[0], rest[1:]
    pulled_ref, grow_ref, ramp_ref = rest[:3]
    if split:
        terms, rest = rest[3 : 3 + count], rest[3 + count :]
    else:
        terms, rest = [rest[3].at[r] for r in range(count)], rest[4:]
    coefs = rest
    edges = query_ref.shape[0]
    wide, span = negs[0].shape
    blocks = edges // step
    if first:
        pulled_ref[...] = jnp.zeros_like(pulled_ref)
        grow_ref[...] = jnp.zeros_like(grow_ref)
        ramp_ref[...] = jnp.zeros_like(ramp_ref)
    else:
        pulled_ref[...] = pulled_in[...]
        grow_ref[...] = grow_in[...]
        ramp_ref[...] = ramp_in[...]

    def score(r, b):
        return jnp.dot(query_ref[b * step : (b + 1) * step, :wide], negs[r][...], preferred_element_type=F32)

    def pull(r, b):
        at = slice(b * step, (b + 1) * step)
        pulled_ref[:, at] += lax.dot_general(negs[r][...], coefs[r % 2][at, :], NT, preferred_element_type=F32)

    def push(r, half):
        at = slice(half * span // 2, (half + 1) * span // 2)
        term = jnp.dot(turned_ref[...], coefs[r % 2][:, at], preferred_element_type=F32)
        if base:
            term = term + base_ref[r, :, at].astype(F32)
        terms[r][:, at] = term.astype(terms[r].dtype)

    units = [(r, b) for r in range(count) for b in range(blocks)]
    gap = score(*units[0])
    for i, (r, b) in enumerate(units):
        after = score(*units[i + 1]) if i + 1 < len(units) else None
        weigh(gap, coefs[r % 2], pl.ds(b * step, step), grow_ref, ramp_ref, weight_ref)
        if r > 0:
            pull(r - 1, b)
            if b % (blocks // 2) == blocks // 2 - 1:
                push(r - 1, b // (blocks // 2))
        gap = after
    for b in range(blocks):
        pull(count - 1, b)
    push(count - 1, 0)
    push(count - 1, 1)


def score_call(query, turned, weight, negs, carry, base, split):
    edges = query.shape[0]
    wide, span = negs[0].shape
    width = turned.shape[0]
    count = len(negs)
    first = carry is None
    ins = [query, turned, weight, *negs] + ([] if first else list(carry)) + ([] if base is None else [base])
    outs = (
        jax.ShapeDtypeStruct((wide, edges), F32),
        jax.ShapeDtypeStruct((edges, LANES), F32),
        jax.ShapeDtypeStruct((edges, LANES), F32),
    )
    if split:
        outs += (jax.ShapeDtypeStruct((width, span), BF),) * count
    else:
        outs += (jax.ShapeDtypeStruct((count, width, span), F32),)
    got = pl.pallas_call(
        functools.partial(score_kernel, first, base is not None, split, count, 256),
        out_shape=outs,
        in_specs=whole(len(ins)),
        out_specs=tuple(whole(len(outs))),
        scratch_shapes=[pltpu.VMEM((edges, span), BF)] * 2,
        compiler_params=pltpu.CompilerParams(vmem_limit_bytes=VMEM_LIMIT),
        cost_estimate=pl.CostEstimate(flops=1, bytes_accessed=1, transcendentals=0),
    )(*ins)
    return got[:3], got[3:] if split else got[3]


def back_kernel(slots, rel_ref, recv_ref, pulled_ref, turned_ref, *refs):
    pair_ref, far_0, far_1, far_2, far_3, near_2, send_ref, side_ref, joined_ref = refs
    side_ref[...] = (far_0[...].astype(F32) + far_1[...].astype(F32) + far_3[...].astype(F32)).astype(BF)
    joined_ref[...] = (near_2[...].astype(F32) + far_2[...].astype(F32)).astype(BF)
    tiles, width = rel_ref.shape[:2]
    for t in range(tiles):
        at = slice(t * LANES, (t + 1) * LANES)
        dst = end_block(recv_ref, slots[2 * t + 1]).astype(F32)
        pulled = pulled_ref[:, at] + pair_ref[:, at]
        total = pulled[width : width + 1]
        grad = (pulled[:width] - total * dst).astype(BF)
        src_term = jnp.dot(rel_ref[t], grad, preferred_element_type=F32)
        dst_term = -total * turned_ref[:, at].astype(F32)
        for end, term in ((0, src_term), (1, dst_term)):
            slot = slots[2 * t + end]
            there = pl.ds(pl.multiple_of(slot % 2 * LANES, LANES), LANES)
            send_ref[slot // 2, :, there] = term.astype(BF)


def place_kernel(need_ref, term_ref, out_ref):
    rows = out_ref.shape[1]
    total = jnp.zeros(out_ref.shape, F32)
    for g in range(need_ref.shape[0]):
        total = total + lax.dot_general(term_ref[g], one_hot(rows, need_ref[g]), NT, preferred_element_type=F32)
    out_ref[...] = total


def span_kernel(neg_ref, *refs):
    out_ref = refs[-1]
    total = refs[0][...].astype(F32)
    for ref in refs[1:-1]:
        total = total + ref[...].astype(F32)
    high = total.astype(BF)
    low = (total - high.astype(F32)).astype(BF)
    hot = one_hot(out_ref.shape[1], neg_ref[...])
    out_ref[...] = lax.dot_general(high, hot, NT, preferred_element_type=F32) + lax.dot_general(
        low, hot, NT, preferred_element_type=F32
    )


def across_z(value, shift):
    pairs = []
    for i in range(16):
        z = (i >> 1) & 3
        pairs.append((i, (i & 9) | (((z + shift) % 4) << 1)))
    return lax.ppermute(value, "blk", pairs)


def across_x(value):
    return lax.ppermute(value, "blk", [(i, i ^ 8) for i in range(16)])


def across_core(value):
    return lax.ppermute(value, "blk", [(i, i ^ 1) for i in range(16)])


def on_device(
    entities, relations, tile_blocks, src_offset, dst_offset, tile_relation, tile_valid, neg_index
):
    ent_dev, width = entities.shape
    tiles, tile = src_offset.shape
    edges = tiles * tile
    ends = 2 * tiles
    doms = lax.axis_size("dom")
    span = neg_index.shape[0]
    negs_count = span * lax.axis_size("blk")
    wide = width + EXTRA
    params = pltpu.CompilerParams(vmem_limit_bytes=8 << 20)
    wide_params = pltpu.CompilerParams(vmem_limit_bytes=14 << 20)

    named = tile_blocks.reshape(ends)
    order = jnp.arange(ends)
    earlier = (named[None, :] == named[:, None]) & (order[None, :] < order[:, None])
    slots = 2 * named + jnp.sum(earlier.astype(jnp.int32), axis=1)
    offsets = jnp.stack([src_offset, dst_offset], axis=1).reshape(ends, tile)
    chosen = slots[None, :] == order[:, None]
    wanted = jnp.sum(jnp.where(chosen[:, :, None], offsets[None], 0), axis=1)
    need = lax.all_to_all(wanted.reshape(doms, 1, 2 * tile), "dom", 0, 0)

    wanted, neg_index = lax.optimization_barrier((wanted, neg_index))
    live = tile_valid.astype(F32)
    pair_live = across_core(live)
    neg_row = neg_index.reshape(1, span)
    turned_ent = entities.T
    own = pl.pallas_call(
        own_kernel,
        out_shape=jax.ShapeDtypeStruct((wide, span), BF),
        in_specs=whole(2),
        out_specs=whole(1)[0],
        compiler_params=params,
    )(turned_ent, neg_row)

    side = across_x(own)
    near = [own] + [across_z(own, -r) for r in (1, 2, 3)]

    in_smem = pl.BlockSpec(memory_space=pltpu.SMEM)
    send = pl.pallas_call(
        pick_kernel,
        out_shape=jax.ShapeDtypeStruct((doms, width, 2 * tile), BF),
        in_specs=whole(2),
        out_specs=whole(1)[0],
        compiler_params=params,
        cost_estimate=pl.CostEstimate(flops=K2_FLOPS, bytes_accessed=1 << 23, transcendentals=0),
    )(turned_ent, need)
    send, side, near[2] = lax.optimization_barrier((send, side, near[2]))
    recv = lax.all_to_all(send, "dom", 0, 0)
    far = [side, across_z(side, -1), across_x(near[2]), across_z(side, -3)]
    recv, near[1], near[3], *far[1:] = lax.optimization_barrier((recv, near[1], near[3], *far[1:]))
    query, turned, weight, pair_weight, own_rels = pl.pallas_call(
        functools.partial(query_kernel, 1.0 / math.sqrt(negs_count)),
        out_shape=(
            jax.ShapeDtypeStruct((edges, 4 * LANES), BF),
            jax.ShapeDtypeStruct((width, edges), BF),
            jax.ShapeDtypeStruct((edges, LANES), F32),
            jax.ShapeDtypeStruct((edges, LANES), F32),
            jax.ShapeDtypeStruct((tiles, width, width), BF),
        ),
        in_specs=[in_smem, in_smem, pl.BlockSpec(memory_space=pl.ANY)] + whole(3),
        out_specs=tuple(whole(5)),
        scratch_shapes=[pltpu.SemaphoreType.DMA((tiles,))],
        compiler_params=pltpu.CompilerParams(vmem_limit_bytes=K3_LIMIT),
        cost_estimate=pl.CostEstimate(flops=1, bytes_accessed=1, transcendentals=0),
    )(tile_relation, slots, relations, recv, live, pair_live)

    pair_query, pair_turned = across_core(query), across_core(turned)
    carry, far_terms = score_call(query, turned, weight, far, None, None, False)
    pair_carry, far_sums = score_call(pair_query, pair_turned, pair_weight, far, None, far_terms, True)
    far_1, far_2, far_3 = across_z(far_sums[1], 1), across_x(far_sums[2]), across_z(far_sums[3], 3)
    pair_carry, near_terms = score_call(pair_query, pair_turned, pair_weight, near, pair_carry, None, False)
    pair_pulled = across_core(pair_carry[0])
    pair_loss = across_core(jnp.sum(jnp.log1p(pair_carry[1]) + pair_carry[2], axis=1).reshape(tiles, tile))
    carry, near_sums = score_call(query, turned, weight, near, carry, near_terms, True)
    pulled, grow, ramp = carry
    terms, side_sum, joined = pl.pallas_call(
        back_kernel,
        out_shape=(jax.ShapeDtypeStruct((doms, width, 2 * tile), BF),)
        + (jax.ShapeDtypeStruct((width, span), BF),) * 2,
        in_specs=[in_smem] + whole(10),
        out_specs=tuple(whole(3)),
        compiler_params=wide_params,
    )(slots, own_rels, recv, pulled, turned, pair_pulled, far_sums[0], far_1, far_2, far_3, near_sums[2])
    terms, side_sum, joined, *near_sums = lax.optimization_barrier((terms, side_sum, joined, *near_sums))
    back = lax.all_to_all(terms, "dom", 0, 0)
    from_side = across_x(side_sum)
    parts = [from_side, near_sums[0], across_z(joined, 2), across_z(near_sums[1], 1), across_z(near_sums[3], 3)]

    positive_grad = pl.pallas_call(
        place_kernel,
        out_shape=jax.ShapeDtypeStruct((width, ent_dev), F32),
        in_specs=whole(2),
        out_specs=whole(1)[0],
        compiler_params=params,
    )(need, back)

    positive_grad, *parts = lax.optimization_barrier((positive_grad, *parts))
    negative_grad = pl.pallas_call(
        span_kernel,
        out_shape=jax.ShapeDtypeStruct((width, ent_dev), F32),
        in_specs=whole(1 + len(parts)),
        out_specs=whole(1)[0],
        compiler_params=params,
    )(neg_row, *parts)

    loss = jnp.sum(jnp.log1p(grow) + ramp, axis=1).reshape(tiles, tile) + pair_loss
    edge_loss = live * (loss / negs_count)
    return (edge_loss, positive_grad.T, negative_grad.T)


def solution(mesh):
    placed = (
        P(("blk", "dom"), None),
        P(),
        P(("blk", "dom"), None),
        P(("blk", "dom"), None),
        P(("blk", "dom"), None),
        P(("blk", "dom")),
        P(("blk", "dom"), None),
        P(("blk", "dom")),
    )
    return jax.shard_map(
        on_device,
        mesh=mesh,
        in_specs=placed,
        out_specs=(P(("blk", "dom"), None), P(("blk", "dom"), None), P(("blk", "dom"), None)),
        check_vma=False,
    )
```

```python
import functools
import math

import jax
import jax.numpy as jnp
from jax import lax
from jax.experimental import pallas as pl
from jax.experimental.pallas import tpu as pltpu
from jax.sharding import PartitionSpec as P

BF = jnp.bfloat16
F32 = jnp.float32
LOG2E = math.log2(math.e)
LANES = 128
VMEM_LIMIT = 18 << 20
K3_LIMIT = 46 << 20
K2_FLOPS = 1 << 33
EXTRA = 16
NT = (((1,), (1,)), ((), ()))


def whole(count):
    return [pl.BlockSpec(memory_space=pltpu.VMEM)] * count


def one_hot(rows, index_row):
    place = lax.broadcasted_iota(jnp.int32, (rows, index_row.shape[1]), 0)
    return jnp.where(place == index_row, 1.0, 0.0).astype(BF)


def own_kernel(ent_ref, neg_ref, own_ref):
    width, rows = ent_ref.shape
    picked = jnp.dot(ent_ref[...], one_hot(rows, neg_ref[...]), preferred_element_type=F32)
    own_ref[:width, :] = picked.astype(BF)
    line = lax.broadcasted_iota(jnp.int32, (EXTRA, own_ref.shape[1]), 0)
    own_ref[width:, :] = jnp.where(line < 2, 1.0, 0.0).astype(BF)


def pick_kernel(turned_ref, need_ref, send_ref):
    rows = turned_ref.shape[1]
    for g in range(need_ref.shape[0]):
        hot = one_hot(rows, need_ref[g])
        send_ref[g] = jnp.dot(turned_ref[...], hot, preferred_element_type=F32).astype(BF)


def end_block(ref, slot):
    return ref[slot // 2, :, pl.ds(pl.multiple_of(slot % 2 * LANES, LANES), LANES)]


def query_kernel(scale, rel_id, slots, rel_ref, recv_ref, valid_ref, pair_ref, query_ref, turned_ref, *refs):
    weight_refs, own_ref, sems = refs[:2], refs[2], refs[3]
    tiles, width = own_ref.shape[:2]
    loads = [pltpu.make_async_copy(rel_ref.at[rel_id[t]], own_ref.at[t], sems.at[t]) for t in range(tiles)]
    for load in loads:
        load.start()
    for live_ref, weight_ref in zip((valid_ref, pair_ref), weight_refs):
        weight = live_ref[...] * scale
        for t in range(tiles):
            at = slice(t * LANES, (t + 1) * LANES)
            weight_ref[at, :] = jnp.broadcast_to(weight[t : t + 1, :], (LANES, LANES)).T
    sources = [end_block(recv_ref, slots[2 * t]).astype(F32).T.astype(BF) for t in range(tiles)]
    for load in loads:
        load.wait()
    line = lax.broadcasted_iota(jnp.int32, (EXTRA, LANES), 0)
    rest = jnp.zeros((query_ref.shape[1] - width - EXTRA, LANES), F32)
    for t in range(tiles):
        at = slice(t * LANES, (t + 1) * LANES)
        dst = end_block(recv_ref, slots[2 * t + 1]).astype(F32)
        query = jnp.dot(sources[t], own_ref[t], preferred_element_type=F32).astype(BF).astype(F32).T
        positive = jnp.sum(query * dst, axis=0, keepdims=True).astype(BF).astype(F32)
        turned_ref[:, at] = query.astype(BF)
        extra = jnp.where(line == 0, -positive, jnp.where(line == 1, 1.0, 0.0))
        query_ref[at, :] = jnp.concatenate([query, extra, rest], axis=0).T.astype(BF)


def weigh(gap, coef_ref, rows, grow_ref, ramp_ref, weight_ref):
    grow, ramp, weight = grow_ref[rows, :], ramp_ref[rows, :], weight_ref[rows, :]
    for k in range(gap.shape[1] // LANES):
        x = gap[:, k * LANES : (k + 1) * LANES]
        e = jnp.exp2(jnp.abs(x) * (-LOG2E))
        d = 1.0 + e
        coef = jnp.where(x >= 0, 1.0, e) / d * weight
        coef_ref[rows, k * LANES : (k + 1) * LANES] = coef.astype(BF)
        ramp = ramp + jnp.maximum(x, 0.0)
        grow = grow * d + e
    grow_ref[rows, :] = grow
    ramp_ref[rows, :] = ramp


def score_kernel(first, base, split, count, step, *refs):
    query_ref, turned_ref, weight_ref = refs[:3]
    negs = refs[3 : 3 + count]
    rest = refs[3 + count :]
    if not first:
        pulled_in, grow_in, ramp_in = rest[:3]
        rest = rest[3:]
    if base:
        base_ref, rest = rest[0], rest[1:]
    pulled_ref, grow_ref, ramp_ref = rest[:3]
    if split:
        terms, rest = rest[3 : 3 + count], rest[3 + count :]
    else:
        terms, rest = [rest[3].at[r] for r in range(count)], rest[4:]
    coefs = rest
    edges = query_ref.shape[0]
    wide, span = negs[0].shape
    blocks = edges // step
    if first:
        pulled_ref[...] = jnp.zeros_like(pulled_ref)
        grow_ref[...] = jnp.zeros_like(grow_ref)
        ramp_ref[...] = jnp.zeros_like(ramp_ref)
    else:
        pulled_ref[...] = pulled_in[...]
        grow_ref[...] = grow_in[...]
        ramp_ref[...] = ramp_in[...]

    def score(r, b):
        return jnp.dot(query_ref[b * step : (b + 1) * step, :wide], negs[r][...], preferred_element_type=F32)

    def pull(r, b):
        at = slice(b * step, (b + 1) * step)
        pulled_ref[:, at] += lax.dot_general(negs[r][...], coefs[r % 2][at, :], NT, preferred_element_type=F32)

    def push(r, half):
        at = slice(half * span // 2, (half + 1) * span // 2)
        term = jnp.dot(turned_ref[...], coefs[r % 2][:, at], preferred_element_type=F32)
        if base:
            term = term + base_ref[r, :, at].astype(F32)
        terms[r][:, at] = term.astype(terms[r].dtype)

    units = [(r, b) for r in range(count) for b in range(blocks)]
    gap = score(*units[0])
    for i, (r, b) in enumerate(units):
        after = score(*units[i + 1]) if i + 1 < len(units) else None
        weigh(gap, coefs[r % 2], pl.ds(b * step, step), grow_ref, ramp_ref, weight_ref)
        if r > 0:
            pull(r - 1, b)
            if b % (blocks // 2) == blocks // 2 - 1:
                push(r - 1, b // (blocks // 2))
        gap = after
    for b in range(blocks):
        pull(count - 1, b)
    push(count - 1, 0)
    push(count - 1, 1)


def score_call(query, turned, weight, negs, carry, base, split):
    edges = query.shape[0]
    wide, span = negs[0].shape
    width = turned.shape[0]
    count = len(negs)
    first = carry is None
    ins = [query, turned, weight, *negs] + ([] if first else list(carry)) + ([] if base is None else [base])
    outs = (
        jax.ShapeDtypeStruct((wide, edges), F32),
        jax.ShapeDtypeStruct((edges, LANES), F32),
        jax.ShapeDtypeStruct((edges, LANES), F32),
    )
    if split:
        outs += (jax.ShapeDtypeStruct((width, span), BF),) * count
    else:
        outs += (jax.ShapeDtypeStruct((count, width, span), F32),)
    got = pl.pallas_call(
        functools.partial(score_kernel, first, base is not None, split, count, 256),
        out_shape=outs,
        in_specs=whole(len(ins)),
        out_specs=tuple(whole(len(outs))),
        scratch_shapes=[pltpu.VMEM((edges, span), BF)] * 2,
        compiler_params=pltpu.CompilerParams(vmem_limit_bytes=VMEM_LIMIT),
        cost_estimate=pl.CostEstimate(flops=1, bytes_accessed=1, transcendentals=0),
    )(*ins)
    return got[:3], got[3:] if split else got[3]


def back_kernel(slots, rel_ref, recv_ref, pulled_ref, turned_ref, *refs):
    pair_ref, far_0, far_1, far_2, far_3, near_2, send_ref, side_ref, joined_ref = refs
    side_ref[...] = (far_0[...].astype(F32) + far_1[...].astype(F32) + far_3[...].astype(F32)).astype(BF)
    joined_ref[...] = (near_2[...].astype(F32) + far_2[...].astype(F32)).astype(BF)
    tiles, width = rel_ref.shape[:2]
    for t in range(tiles):
        at = slice(t * LANES, (t + 1) * LANES)
        dst = end_block(recv_ref, slots[2 * t + 1]).astype(F32)
        pulled = pulled_ref[:, at] + pair_ref[:, at]
        total = pulled[width : width + 1]
        grad = (pulled[:width] - total * dst).astype(BF)
        src_term = jnp.dot(rel_ref[t], grad, preferred_element_type=F32)
        dst_term = -total * turned_ref[:, at].astype(F32)
        for end, term in ((0, src_term), (1, dst_term)):
            slot = slots[2 * t + end]
            there = pl.ds(pl.multiple_of(slot % 2 * LANES, LANES), LANES)
            send_ref[slot // 2, :, there] = term.astype(BF)


def place_kernel(need_ref, term_ref, out_ref):
    rows = out_ref.shape[1]
    total = jnp.zeros(out_ref.shape, F32)
    for g in range(need_ref.shape[0]):
        total = total + lax.dot_general(term_ref[g], one_hot(rows, need_ref[g]), NT, preferred_element_type=F32)
    out_ref[...] = total


def span_kernel(neg_ref, *refs):
    out_ref = refs[-1]
    total = refs[0][...].astype(F32)
    for ref in refs[1:-1]:
        total = total + ref[...].astype(F32)
    high = total.astype(BF)
    low = (total - high.astype(F32)).astype(BF)
    hot = one_hot(out_ref.shape[1], neg_ref[...])
    out_ref[...] = lax.dot_general(high, hot, NT, preferred_element_type=F32) + lax.dot_general(
        low, hot, NT, preferred_element_type=F32
    )


def across_z(value, shift):
    pairs = []
    for i in range(16):
        z = (i >> 1) & 3
        pairs.append((i, (i & 9) | (((z + shift) % 4) << 1)))
    return lax.ppermute(value, "blk", pairs)


def across_x(value):
    return lax.ppermute(value, "blk", [(i, i ^ 8) for i in range(16)])


def across_core(value):
    return lax.ppermute(value, "blk", [(i, i ^ 1) for i in range(16)])


def on_device(
    entities, relations, tile_blocks, src_offset, dst_offset, tile_relation, tile_valid, neg_index
):
    ent_dev, width = entities.shape
    tiles, tile = src_offset.shape
    edges = tiles * tile
    ends = 2 * tiles
    doms = lax.axis_size("dom")
    span = neg_index.shape[0]
    negs_count = span * lax.axis_size("blk")
    wide = width + EXTRA
    params = pltpu.CompilerParams(vmem_limit_bytes=8 << 20)
    wide_params = pltpu.CompilerParams(vmem_limit_bytes=14 << 20)

    named = tile_blocks.reshape(ends)
    order = jnp.arange(ends)
    earlier = (named[None, :] == named[:, None]) & (order[None, :] < order[:, None])
    slots = 2 * named + jnp.sum(earlier.astype(jnp.int32), axis=1)
    offsets = jnp.stack([src_offset, dst_offset], axis=1).reshape(ends, tile)
    chosen = slots[None, :] == order[:, None]
    wanted = jnp.sum(jnp.where(chosen[:, :, None], offsets[None], 0), axis=1)
    need = lax.all_to_all(wanted.reshape(doms, 1, 2 * tile), "dom", 0, 0)

    wanted, neg_index = lax.optimization_barrier((wanted, neg_index))
    live = tile_valid.astype(F32)
    pair_live = across_core(live)
    neg_row = neg_index.reshape(1, span)
    turned_ent = entities.T
    own = pl.pallas_call(
        own_kernel,
        out_shape=jax.ShapeDtypeStruct((wide, span), BF),
        in_specs=whole(2),
        out_specs=whole(1)[0],
        compiler_params=params,
    )(turned_ent, neg_row)

    side = across_x(own)
    near = [own] + [across_z(own, -r) for r in (1, 2, 3)]

    in_smem = pl.BlockSpec(memory_space=pltpu.SMEM)
    send = pl.pallas_call(
        pick_kernel,
        out_shape=jax.ShapeDtypeStruct((doms, width, 2 * tile), BF),
        in_specs=whole(2),
        out_specs=whole(1)[0],
        compiler_params=params,
        cost_estimate=pl.CostEstimate(flops=K2_FLOPS, bytes_accessed=1 << 23, transcendentals=0),
    )(turned_ent, need)
    send, side, near[2] = lax.optimization_barrier((send, side, near[2]))
    recv = lax.all_to_all(send, "dom", 0, 0)
    far = [side, across_z(side, -1), across_x(near[2]), across_z(side, -3)]
    recv, near[1], near[3], *far[1:] = lax.optimization_barrier((recv, near[1], near[3], *far[1:]))
    query, turned, weight, pair_weight, own_rels = pl.pallas_call(
        functools.partial(query_kernel, 1.0 / math.sqrt(negs_count)),
        out_shape=(
            jax.ShapeDtypeStruct((edges, 4 * LANES), BF),
            jax.ShapeDtypeStruct((width, edges), BF),
            jax.ShapeDtypeStruct((edges, LANES), F32),
            jax.ShapeDtypeStruct((edges, LANES), F32),
            jax.ShapeDtypeStruct((tiles, width, width), BF),
        ),
        in_specs=[in_smem, in_smem, pl.BlockSpec(memory_space=pl.ANY)] + whole(3),
        out_specs=tuple(whole(5)),
        scratch_shapes=[pltpu.SemaphoreType.DMA((tiles,))],
        compiler_params=pltpu.CompilerParams(vmem_limit_bytes=K3_LIMIT),
        cost_estimate=pl.CostEstimate(flops=1, bytes_accessed=1, transcendentals=0),
    )(tile_relation, slots, relations, recv, live, pair_live)

    pair_query, pair_turned = across_core(query), across_core(turned)
    carry, far_terms = score_call(query, turned, weight, far, None, None, False)
    pair_carry, far_sums = score_call(pair_query, pair_turned, pair_weight, far, None, far_terms, True)
    far_1, far_2, far_3 = across_z(far_sums[1], 1), across_x(far_sums[2]), across_z(far_sums[3], 3)
    pair_carry, near_terms = score_call(pair_query, pair_turned, pair_weight, near, pair_carry, None, False)
    pair_pulled = across_core(pair_carry[0])
    pair_loss = across_core(jnp.sum(jnp.log1p(pair_carry[1]) + pair_carry[2], axis=1).reshape(tiles, tile))
    carry, near_sums = score_call(query, turned, weight, near, carry, near_terms, True)
    pulled, grow, ramp = carry
    terms, side_sum, joined = pl.pallas_call(
        back_kernel,
        out_shape=(jax.ShapeDtypeStruct((doms, width, 2 * tile), BF),)
        + (jax.ShapeDtypeStruct((width, span), BF),) * 2,
        in_specs=[in_smem] + whole(10),
        out_specs=tuple(whole(3)),
        compiler_params=wide_params,
    )(slots, own_rels, recv, pulled, turned, pair_pulled, far_sums[0], far_1, far_2, far_3, near_sums[2])
    terms, side_sum, joined, near_1, near_3 = lax.optimization_barrier((terms, side_sum, joined, near_sums[1], near_sums[3]))
    back = lax.all_to_all(terms, "dom", 0, 0)
    from_side = across_x(side_sum)
    parts = [from_side, near_sums[0], across_z(joined, 2), across_z(near_1, 1), across_z(near_3, 3)]

    positive_grad = pl.pallas_call(
        place_kernel,
        out_shape=jax.ShapeDtypeStruct((width, ent_dev), F32),
        in_specs=whole(2),
        out_specs=whole(1)[0],
        compiler_params=params,
    )(need, back)

    positive_grad, *parts = lax.optimization_barrier((positive_grad, *parts))
    negative_grad = pl.pallas_call(
        span_kernel,
        out_shape=jax.ShapeDtypeStruct((width, ent_dev), F32),
        in_specs=whole(1 + len(parts)),
        out_specs=whole(1)[0],
        compiler_params=params,
    )(neg_row, *parts)

    loss = jnp.sum(jnp.log1p(grow) + ramp, axis=1).reshape(tiles, tile) + pair_loss
    edge_loss = live * (loss / negs_count)
    return (edge_loss, positive_grad.T, negative_grad.T)


def solution(mesh):
    placed = (
        P(("blk", "dom"), None),
        P(),
        P(("blk", "dom"), None),
        P(("blk", "dom"), None),
        P(("blk", "dom"), None),
        P(("blk", "dom")),
        P(("blk", "dom"), None),
        P(("blk", "dom")),
    )
    return jax.shard_map(
        on_device,
        mesh=mesh,
        in_specs=placed,
        out_specs=(P(("blk", "dom"), None), P(("blk", "dom"), None), P(("blk", "dom"), None)),
        check_vma=False,
    )
```
